32 devices in a mesh: groups: 1, expert: 16 (over z, y, x), tower: 2 (over core).
Axes of the slice: x: 2, y: 2, z: 4, core: 2. Of those that a mesh axis runs over, the one named last changes fastest.
Arguments:
- output_grad: bfloat16 [2048, 4096], P(('groups', 'expert'), 'tower'), may hold values from -6 to 6
- gate_values: float32 [2048, 8], P(('groups', 'expert')), may hold values from 0.05 to 0.25
- expert_ids: int32 [2048, 8], P(('groups', 'expert')), may hold values from 0 to 15, all different within a row; in each aligned block of 128 rows (0 to 127, 128 to 255, ...) at most 112 rows name the same one
- pre_gate: bfloat16 [16, 16, 112, 768], P(('groups', 'expert')), may hold values from -6 to 6
- pre_up: bfloat16 [16, 16, 112, 768], P(('groups', 'expert')), may hold values from -6 to 6
- w_gate: bfloat16 [16, 4096, 768], P('expert', 'tower'), may hold values from -0.21875 to 0.21875
- w_up: bfloat16 [16, 4096, 768], P('expert', 'tower'), may hold values from -0.21875 to 0.21875
- w_down: bfloat16 [16, 768, 4096], P('expert', None, 'tower'), may hold values from -0.09375 to 0.09375
- visual: bfloat16 [256, 1152], P(('groups', 'expert')), may hold values from -0.5 to 0.5
- visual_rows: int32 [256], P(('groups', 'expert')), may hold values from 0 to 127
Outputs:
- input_grad: bfloat16 [2048, 4096], P(('groups', 'expert'), 'tower')
- projector_grad: float32 [1152, 4096], P(('groups', 'expert'), 'tower')
The draws below stay inside these ranges and needn't reach their ends.
Inputs may be any that keep to these rules, and one draw needn't show every extreme that they name: `expert_ids`: each row names 8 different experts. Among the tokens of one block no expert is named by more than 112 rows, a bound that some block reaches. `visual_rows`: rows may repeat.
All inputs are finite; a program needn't handle non-finite values.
Results may differ from the reference program's by a relative error of at most 0.0033.
Values may be sent and summed in bfloat16 or wider, within the bound.
A program may use at most 128 MiB of HBM per device.

```python
import math
import jax
import jax.numpy as jnp
import numpy as np
from jax import lax

D = 4096
TOPK = 8
FF = 768
VW = 1152
TOK_E = 128
VIS_E = 16
EXPERTS = 16
BLOCKS = 16
TOKENS = 2048
VIS = 256
CAP = 112


def with_ends(values, key, smallest, top_value):
    extent = values.shape
    index_at = [jax.random.randint(jax.random.fold_in(key, axis), (), 0, extent[axis]) for axis in range(len(extent))]
    values = values.at[tuple(index_at)].set(smallest)
    longest = extent.index(max(extent))
    index_at[longest] = (index_at[longest] + 1) % extent[longest]
    return values.at[tuple(index_at)].set(top_value)


def with_spikes(drawn, stream_key, source, target, shards_of, factor):
    owner, partner = [(jnp.arange(drawn.shape[dim]) // (drawn.shape[dim] // shards_of)).reshape([-1 if axis == dim else 1 for axis in range(drawn.ndim)]) for dim in (source, target)]
    chosen = jax.random.permutation(stream_key, shards_of)[partner]
    strong = (owner == chosen) | (owner == (partner + shards_of // 2) % shards_of)
    return jnp.where(strong, factor * drawn, drawn)


def block_levels(own_key, dims, split, low, high):
    factor_of = 1.0
    for dim, parts in split:
        heights = jax.random.uniform(jax.random.fold_in(jax.random.fold_in(own_key, 6), dim), (parts,), jnp.float32, low / len(split), high / len(split))
        factor_of = factor_of * jnp.repeat(jnp.exp(heights), dims[dim] // parts).reshape((-1,) + (1,) * (len(dims) - 1 - dim))
    return factor_of


def deal_out(key, own, number, rows, amount, top, reach, skew):
    order = jax.random.permutation(key, amount)
    packed, usual = portions_of(amount, rows * top, reach, skew, True), portions_of(amount, rows * top, reach, skew, False)
    places = jnp.arange(amount)

    def named(sizes, turn):
        used = int((sizes > 0).sum())
        fixed = max(1, used // 4)
        passed = fixed + (places - fixed + turn * (used - fixed)) % max(1, amount - fixed)
        return jnp.zeros((amount,), jnp.int32).at[order[jnp.where(places < fixed, places, passed)]].set(jnp.asarray(sizes, jnp.int32))

    sizes = jnp.where(number % 4 == 0, named(packed, number // 4), named(usual, number - number // 4 - 1))
    mixed = jax.random.permutation(jax.random.fold_in(own, 3), amount)
    donor, taker = mixed[0:amount // 2 * 2:2], mixed[1:amount // 2 * 2:2]
    room = jnp.minimum(sizes[donor] - 1, reach - sizes[taker]) // 2
    room = jnp.where((donor == order[0]) | (taker == order[0]) | (sizes[taker] == 0), 0, jnp.maximum(room, 0))
    passed = jax.random.randint(jax.random.fold_in(own, 4), (amount // 2,), 0, 1 << 20) % (room + 1)
    sizes = sizes.at[donor].add(-passed).at[taker].add(passed)
    labels = jnp.searchsorted(jnp.cumsum(sizes), jnp.arange(rows * top), side="right").astype(jnp.int32)
    listing = labels.reshape(top, rows).T
    listing = listing[jax.random.permutation(jax.random.fold_in(own, 1), rows)]
    turn = jax.random.randint(jax.random.fold_in(own, 2), (rows, 1), 0, top)
    return jnp.take_along_axis(listing, (jnp.arange(top)[None, :] + turn) % top, axis=1)


def portions_of(count, total, limit, skew, full):
    portions = [(1 << 20) // math.isqrt(rank ** skew) + 1 for rank in range(1, count + 1)]
    largest = limit if full else min(limit, max(-(-total // count), total * portions[0] // sum(portions)))
    least = 1 if total - largest >= count - 1 else 0
    holding, rest = [largest] + [least] * (count - 1), total - largest - least * (count - 1)
    while rest > 0:
        movable = [i for i in range(1, count) if holding[i] < largest] or [i for i in range(1, count) if holding[i] < limit]
        mass, budget = sum([portions[i] for i in movable]), rest
        for i in movable:
            extra = min(limit - holding[i], max(1, budget * portions[i] // mass), rest)
            holding[i] = holding[i] + extra
            rest = rest - extra
    return np.array(holding)


def gaussian(stream_key, dims, spread, reach, pieces=(), kind=jnp.bfloat16):
    factor_of = block_levels(stream_key, dims, pieces, -0.22, 0.18) if pieces else 1.0
    drawn = jax.random.normal(stream_key, dims, jnp.float32) * spread * factor_of
    return jnp.minimum(jnp.maximum(drawn, -reach), reach).astype(kind)


def gaussian_with(stream_key, shape, width, most, split, heavy, kind=jnp.bfloat16):
    drawn = width * jax.random.normal(stream_key, shape, jnp.float32)
    if split:
        drawn = drawn * block_levels(stream_key, shape, split, -0.22, 0.18)
    return jnp.clip(with_spikes(drawn, jax.random.fold_in(stream_key, 3), *heavy), -most, most).astype(kind)


def setup_inputs(seed: int = 0, part: int = 0) -> dict:
    key_list = jax.random.split(jax.random.key(seed), 11)
    part_keys = jax.random.split(jax.random.fold_in(key_list[10], part), 11)
    output_grad = gaussian(part_keys[0], (TOKENS, D), 1.0, 6.0, ((0, 16), (1, 2)))
    gate_values = jnp.clip(0.05 + 0.2 * jax.random.uniform(part_keys[1], (TOKENS, TOPK), jnp.float32) ** block_levels(part_keys[1], (TOKENS, TOPK), ((0, 16),), -0.2, 0.2), 0.05, 0.25)
    expert_ids_keys = jax.random.split(jax.random.fold_in(part_keys[2], 1), TOKENS // TOK_E)
    expert_ids_turns = jax.random.permutation(jax.random.fold_in(part_keys[2], 3), TOKENS // TOK_E)
    expert_ids = jax.vmap(lambda own, number: deal_out(jax.random.fold_in(part_keys[2], 2), own, number, TOK_E, EXPERTS, TOPK, CAP, 2))(expert_ids_keys, expert_ids_turns).reshape((TOKENS, TOPK))
    pre_gate = gaussian(part_keys[3], (EXPERTS, BLOCKS, CAP, FF), 1.0, 6.0, ((0, 16),))
    pre_up = gaussian(part_keys[4], (EXPERTS, BLOCKS, CAP, FF), 1.0, 6.0, ((0, 16),))
    w_gate = gaussian(key_list[5], (EXPERTS, D, FF), FF ** -0.5, 0.21875, ((0, 16), (1, 2)))
    w_up = gaussian(key_list[6], (EXPERTS, D, FF), FF ** -0.5, 0.21875, ((0, 16), (1, 2)))
    w_down = gaussian(key_list[7], (EXPERTS, FF, D), D ** -0.5, 0.09375, ((0, 16), (2, 2)))
    visual = gaussian_with(part_keys[8], (VIS, VW), (1.0 / VIS ** 0.5), 0.5, ((0, 16),), (0, 1, 16, 2.0))
    visual_rows = with_ends(jax.random.randint(part_keys[9], (VIS,), 0, TOK_E), jax.random.fold_in(part_keys[9], 1), 0, TOK_E - 1).astype(jnp.int32)
    return dict(output_grad=output_grad, gate_values=gate_values, expert_ids=expert_ids, pre_gate=pre_gate, pre_up=pre_up, w_gate=w_gate, w_up=w_up, w_down=w_down, visual=visual, visual_rows=visual_rows)


def slot_positions(expert_ids):
    flat_ids = expert_ids.reshape(BLOCKS, TOK_E * TOPK)
    onehot = (flat_ids[:, :, None] == jnp.arange(EXPERTS, dtype=jnp.int32)[None, None, :]).astype(jnp.int32)
    earlier = jnp.cumsum(onehot, axis=1) - onehot
    return flat_ids, jnp.sum(earlier * onehot, axis=2).astype(jnp.int32)


def hidden_grads(summed, gate_pre, up_pre):
    gate_float = gate_pre.astype(jnp.float32)
    up_float = up_pre.astype(jnp.float32)
    sigmoid_gate = jax.nn.sigmoid(gate_float)
    slope = sigmoid_gate * (1.0 + gate_float * (1.0 - sigmoid_gate))
    grad_gate = (summed * up_float * slope).astype(jnp.bfloat16)
    grad_up = (summed * gate_float * sigmoid_gate).astype(jnp.bfloat16)
    return grad_gate, grad_up


def reference(output_grad, gate_values, expert_ids, pre_gate, pre_up, w_gate, w_up, w_down, visual, visual_rows):
    flat_ids, position = slot_positions(expert_ids)
    block_index = jnp.arange(BLOCKS, dtype=jnp.int32)[:, None]
    slot_index = ((flat_ids * BLOCKS + block_index) * CAP + position).reshape(-1).astype(jnp.int32)
    token_index = jnp.repeat(jnp.arange(TOKENS, dtype=jnp.int32), TOPK)
    slot_tokens = jnp.full((EXPERTS * BLOCKS * CAP,), -1, jnp.int32).at[slot_index].set(token_index)
    slot_tokens = slot_tokens.reshape(EXPERTS, BLOCKS * CAP)

    def one_expert(inputs):
        tokens_here, gate_pre, up_pre, gate_weight, up_weight, down_weight = inputs
        filled = tokens_here >= 0
        gathered = jnp.where(filled[:, None], output_grad[jnp.maximum(tokens_here, 0)], jnp.zeros((), output_grad.dtype))
        summed = jnp.dot(gathered, down_weight.T, preferred_element_type=jnp.float32)
        grad_gate, grad_up = hidden_grads(summed, gate_pre, up_pre)
        returning = jnp.dot(grad_gate, gate_weight.T, preferred_element_type=jnp.float32)
        returning = returning + jnp.dot(grad_up, up_weight.T, preferred_element_type=jnp.float32)
        return returning.astype(jnp.bfloat16)

    returned = lax.map(one_expert, (slot_tokens, pre_gate.reshape(EXPERTS, BLOCKS * CAP, FF), pre_up.reshape(EXPERTS, BLOCKS * CAP, FF), w_gate, w_up, w_down))
    picked = returned.reshape(EXPERTS * BLOCKS * CAP, D)[slot_index].reshape(TOKENS, TOPK, D)
    combined = output_grad.astype(jnp.float32) + jnp.sum(gate_values[:, :, None] * picked.astype(jnp.float32), axis=1)
    input_grad = combined.astype(jnp.bfloat16)
    visual_token = ((jnp.arange(VIS, dtype=jnp.int32) // VIS_E) * TOK_E + visual_rows).astype(jnp.int32)
    projector_grad = jnp.dot(visual.T, input_grad[visual_token], preferred_element_type=jnp.float32)
    return input_grad, projector_grad
```

```python
import jax
import jax.numpy as jnp
from jax import lax
from jax.sharding import PartitionSpec as P


def hidden_grads(summed, gate_pre, up_pre):
    gate_float = gate_pre.astype(jnp.float32)
    up_float = up_pre.astype(jnp.float32)
    sigmoid_gate = jax.nn.sigmoid(gate_float)
    slope = sigmoid_gate * (1.0 + gate_float * (1.0 - sigmoid_gate))
    grad_gate = (summed * up_float * slope).astype(jnp.bfloat16)
    grad_up = (summed * gate_float * sigmoid_gate).astype(jnp.bfloat16)
    return (grad_gate, grad_up)


def per_device(
    output_grad,
    gate_values,
    expert_ids,
    pre_gate,
    pre_up,
    w_gate,
    w_up,
    w_down,
    visual,
    visual_rows,
):
    tok_rows, half_width = output_grad.shape
    top_count = expert_ids.shape[1]
    expert_count = lax.axis_size("expert")
    capacity = pre_gate.shape[2]
    hidden_units = pre_gate.shape[3]
    flat_ids = expert_ids.reshape(-1)
    onehot = (flat_ids[:, None] == jnp.arange(expert_count, dtype=jnp.int32)[None, :]).astype(
        jnp.int32
    )
    earlier = jnp.cumsum(onehot, axis=0) - onehot
    position = jnp.sum(earlier * onehot, axis=1)
    slot_index = flat_ids * capacity + position
    token_index = jnp.repeat(jnp.arange(tok_rows, dtype=jnp.int32), top_count)
    outgoing = (
        jnp.zeros((expert_count * capacity, half_width), jnp.bfloat16)
        .at[slot_index]
        .set(output_grad[token_index])
    )
    outgoing = outgoing.reshape(expert_count, capacity, half_width)
    incoming = lax.all_to_all(outgoing, "expert", split_axis=0, concat_axis=0, tiled=True)
    routed = incoming.reshape(-1, half_width)
    partial_value = jnp.einsum("rd,fd->rf", routed, w_down[0], preferred_element_type=jnp.float32)
    gate_pre = pre_gate[0].reshape(-1, hidden_units)
    up_pre = pre_up[0].reshape(-1, hidden_units)
    summed = lax.psum(partial_value, "tower")
    grad_gate, grad_up = hidden_grads(summed, gate_pre, up_pre)
    returning = jnp.einsum("rf,df->rd", grad_gate, w_gate[0], preferred_element_type=jnp.float32)
    returning = returning + jnp.einsum(
        "rf,df->rd", grad_up, w_up[0], preferred_element_type=jnp.float32
    )
    returning = returning.astype(jnp.bfloat16).reshape(expert_count, capacity, half_width)
    returned = lax.all_to_all(returning, "expert", split_axis=0, concat_axis=0, tiled=True)
    picked = returned.reshape(-1, half_width)[slot_index].reshape(tok_rows, top_count, half_width)
    combined = output_grad.astype(jnp.float32) + jnp.sum(
        gate_values[:, :, None] * picked.astype(jnp.float32), axis=1
    )
    input_grad = combined.astype(jnp.bfloat16)
    visual_grad = input_grad[visual_rows]
    features = lax.all_to_all(visual, "expert", split_axis=1, concat_axis=0, tiled=True)
    projector_grad = jnp.einsum(
        "rv,rd->vd",
        features,
        lax.all_gather(visual_grad, "expert", axis=0, tiled=True),
        preferred_element_type=jnp.float32,
    )
    return (input_grad, projector_grad)


def per_device_tokens(
    output_grad,
    gate_values,
    expert_ids,
    pre_gate,
    pre_up,
    w_gate,
    w_up,
    w_down,
    visual,
    visual_rows,
):
    tok_rows, half_width = output_grad.shape
    blocks = lax.axis_size("expert")
    capacity, hidden_units = pre_gate.shape[2:]
    me = lax.axis_index("expert")
    every_grad = lax.all_gather(output_grad, "expert", axis=0, tiled=True)
    every_id = lax.all_gather(expert_ids, "expert", axis=0, tiled=True)
    every_value = lax.all_gather(gate_values, "expert", axis=0, tiled=True)
    named = every_id == me
    weight = jnp.sum(jnp.where(named, every_value, 0.0), axis=1)
    here = jnp.any(named, axis=1).reshape(blocks, tok_rows)
    count = here.astype(jnp.int32)
    position = jnp.cumsum(count, axis=1) - count
    position = jnp.where(here, position, -1)
    onehot = (position[:, :, None] == jnp.arange(capacity, dtype=jnp.int32)).astype(jnp.bfloat16)
    gate_pre = jnp.einsum("btc,bcf->btf", onehot, pre_gate[0]).reshape(-1, hidden_units)
    up_pre = jnp.einsum("btc,bcf->btf", onehot, pre_up[0]).reshape(-1, hidden_units)
    partial_value = jnp.einsum(
        "rd,fd->rf", every_grad, w_down[0], preferred_element_type=jnp.float32
    )
    summed = lax.psum(partial_value, "tower")
    grad_gate, grad_up = hidden_grads(summed, gate_pre, up_pre)
    returning = jnp.einsum("rf,df->rd", grad_gate, w_gate[0], preferred_element_type=jnp.float32)
    returning = returning + jnp.einsum(
        "rf,df->rd", grad_up, w_up[0], preferred_element_type=jnp.float32
    )
    returning = (returning * weight[:, None]).astype(jnp.bfloat16)
    total = lax.psum_scatter(returning, "expert", scatter_dimension=0, tiled=True)
    input_grad = (output_grad.astype(jnp.float32) + total.astype(jnp.float32)).astype(jnp.bfloat16)
    return (input_grad, projector(input_grad, visual, visual_rows))


def projector(input_grad, visual, visual_rows):
    visual_grad = input_grad[visual_rows]
    features = lax.all_to_all(visual, "expert", split_axis=1, concat_axis=0, tiled=True)
    return jnp.einsum(
        "rv,rd->vd",
        features,
        lax.all_gather(visual_grad, "expert", axis=0, tiled=True),
        preferred_element_type=jnp.float32,
    )


def solution(mesh):
    per_rank = per_device_tokens if mesh.shape["expert"] <= 16 else per_device
    in_specs = (
        P(("groups", "expert"), "tower"),
        P(("groups", "expert"), None),
        P(("groups", "expert"), None),
        P(("groups", "expert"), None, None, None),
        P(("groups", "expert"), None, None, None),
        P("expert", "tower", None),
        P("expert", "tower", None),
        P("expert", None, "tower"),
        P(("groups", "expert"), None),
        P(("groups", "expert")),
    )
    out_specs = (P(("groups", "expert"), "tower"), P(("groups", "expert"), "tower"))
    return jax.shard_map(
        per_rank, mesh=mesh, in_specs=in_specs, out_specs=out_specs, check_vma=False
    )
```

```python
import jax
import jax.numpy as jnp
from jax import lax
from jax.experimental import pallas as pl
from jax.experimental.pallas import tpu as pltpu
from jax.sharding import PartitionSpec as P


def hidden_grads(summed, gate_pre, up_pre):
    gate_float = gate_pre.astype(jnp.float32)
    up_float = up_pre.astype(jnp.float32)
    sigmoid_gate = jax.nn.sigmoid(gate_float)
    slope = sigmoid_gate * (1.0 + gate_float * (1.0 - sigmoid_gate))
    grad_gate = (summed * up_float * slope).astype(jnp.bfloat16)
    grad_up = (summed * gate_float * sigmoid_gate).astype(jnp.bfloat16)
    return (grad_gate, grad_up)


def per_device(
    output_grad,
    gate_values,
    expert_ids,
    pre_gate,
    pre_up,
    w_gate,
    w_up,
    w_down,
    visual,
    visual_rows,
):
    tok_rows, half_width = output_grad.shape
    top_count = expert_ids.shape[1]
    expert_count = lax.axis_size("expert")
    capacity = pre_gate.shape[2]
    hidden_units = pre_gate.shape[3]
    flat_ids = expert_ids.reshape(-1)
    onehot = (flat_ids[:, None] == jnp.arange(expert_count, dtype=jnp.int32)[None, :]).astype(
        jnp.int32
    )
    earlier = jnp.cumsum(onehot, axis=0) - onehot
    position = jnp.sum(earlier * onehot, axis=1)
    slot_index = flat_ids * capacity + position
    token_index = jnp.repeat(jnp.arange(tok_rows, dtype=jnp.int32), top_count)
    outgoing = (
        jnp.zeros((expert_count * capacity, half_width), jnp.bfloat16)
        .at[slot_index]
        .set(output_grad[token_index])
    )
    outgoing = outgoing.reshape(expert_count, capacity, half_width)
    incoming = lax.all_to_all(outgoing, "expert", split_axis=0, concat_axis=0, tiled=True)
    routed = incoming.reshape(-1, half_width)
    partial_value = jnp.einsum("rd,fd->rf", routed, w_down[0], preferred_element_type=jnp.float32)
    gate_pre = pre_gate[0].reshape(-1, hidden_units)
    up_pre = pre_up[0].reshape(-1, hidden_units)
    summed = lax.psum(partial_value, "tower")
    grad_gate, grad_up = hidden_grads(summed, gate_pre, up_pre)
    returning = jnp.einsum("rf,df->rd", grad_gate, w_gate[0], preferred_element_type=jnp.float32)
    returning = returning + jnp.einsum(
        "rf,df->rd", grad_up, w_up[0], preferred_element_type=jnp.float32
    )
    returning = returning.astype(jnp.bfloat16).reshape(expert_count, capacity, half_width)
    returned = lax.all_to_all(returning, "expert", split_axis=0, concat_axis=0, tiled=True)
    picked = returned.reshape(-1, half_width)[slot_index].reshape(tok_rows, top_count, half_width)
    combined = output_grad.astype(jnp.float32) + jnp.sum(
        gate_values[:, :, None] * picked.astype(jnp.float32), axis=1
    )
    input_grad = combined.astype(jnp.bfloat16)
    visual_grad = input_grad[visual_rows]
    features = lax.all_to_all(visual, "expert", split_axis=1, concat_axis=0, tiled=True)
    projector_grad = jnp.einsum(
        "rv,rd->vd",
        features,
        lax.all_gather(visual_grad, "expert", axis=0, tiled=True),
        preferred_element_type=jnp.float32,
    )
    return (input_grad, projector_grad)


def expert_kernel(
    og, info, pg, pu, wg, wu, wd, out,
    held, contrib, gate_tok, up_tok, own_sum, half_out, half_in, grad_g, grad_u, l1, l2, l3,
    zs, zr, xs, xr, ys, yr, fs, fr, hs, hr, s1, r1, s2, r2, s3, r3,
):
    zl, tok, half = held.shape[2:]
    hid = wd.shape[0]
    cap = pg.shape[2]
    rows = zl * tok
    group, me, core = lax.axis_index("groups"), lax.axis_index("expert"), lax.axis_index("tower")
    z, y, x = lax.div(me, 4), lax.rem(lax.div(me, 2), 2), lax.rem(me, 2)
    q, qx = y * 2 + x, y * 2 + 1 - x
    qy, qd = (1 - y) * 2 + x, (1 - y) * 2 + 1 - x

    def dev(e):
        return (group, e, core)

    xn, yn = dev(z * 4 + qx), dev(z * 4 + qy)
    other = (group, me, 1 - core)
    zto = [lax.rem(z + k, 4) for k in range(4)]
    zfrom = [lax.rem(z + 4 - k, 4) for k in range(4)]
    zdev = [dev(zto[k] * 4 + q) for k in range(4)]

    def remote(src, dst, ss, rs, device):
        return pltpu.make_async_remote_copy(
            src_ref=src, dst_ref=dst, send_sem=ss, recv_sem=rs,
            device_id=device, device_id_type=pl.DeviceIdType.MESH,
        )

    barrier = pltpu.get_barrier_semaphore()
    for device in (xn, yn, other, zdev[1], zdev[2], zdev[3]):
        pl.semaphore_signal(barrier, inc=1, device_id=device, device_id_type=pl.DeviceIdType.MESH)
    for h in range(2):
        held[h, q, z] = og[:, h * half : (h + 1) * half]
    pl.semaphore_wait(barrier, 6)

    started = []

    def go(copy):
        copy.start()
        started.append(copy)
        return copy

    def to_x(k, h):
        block = held.at[h, q, zfrom[k]]
        return go(remote(block, block, xs.at[k, h], xr.at[k, h], xn))

    def to_y(k, h):
        block = held.at[h, q, zfrom[k]]
        return go(remote(block, block, ys.at[k, h], yr.at[k, h], yn))

    zc, xc, yc, fc = {}, {}, {}, {}

    def forward(k):
        xc[k, 0].wait_recv()
        block = held.at[0, qx, zfrom[k]]
        fc[k, 0] = go(remote(block, block, fs.at[k, 0], fr.at[k, 0], yn))
        yc[k, 1].wait_recv()
        block = held.at[1, qy, zfrom[k]]
        fc[k, 1] = go(remote(block, block, fs.at[k, 1], fr.at[k, 1], xn))

    for k in (1, 3, 2):
        for h in range(2):
            block = held.at[h, q, z]
            zc[k, h] = remote(block, block, zs.at[k, h], zr.at[k, h], zdev[k])
    xc[0, 0], yc[0, 1] = to_x(0, 0), to_y(0, 1)
    for k in (1, 3, 2):
        go(zc[k, 0])
        go(zc[k, 1])
    xc[0, 1], yc[0, 0] = to_x(0, 1), to_y(0, 0)

    @pl.loop(0, 4)
    def _(zi):
        @pl.loop(0, 4)
        def _(qi):
            place = info[zi * 4 + qi, :, 1:2]
            slot = lax.broadcasted_iota(jnp.int32, (tok, cap), 1).astype(jnp.float32)
            spread = jnp.where(place == slot, 1.0, 0.0).astype(jnp.bfloat16)
            for pre, dest in ((pg, gate_tok), (pu, up_tok)):
                dest[qi, zi] = jnp.dot(
                    spread, pre[zi, qi], preferred_element_type=jnp.float32
                ).astype(jnp.bfloat16)

    done = None
    for k in (1, 3, 2):
        zc[k, 0].wait_recv()
        xc[k, 0] = to_x(k, 0)
        zc[k, 1].wait_recv()
        yc[k, 1] = to_y(k, 1)
        xc[k, 1], yc[k, 0] = to_x(k, 1), to_y(k, 0)
        forward(0 if done is None else done)
        done = k

    hc = []

    def hidden(g, qq):
        @pl.loop(0, hid // 256)
        def _(n):
            cols = pl.ds(pl.multiple_of(n * 256, 256), 256)
            total = jnp.zeros((rows, 256), jnp.float32)
            for h in range(2):
                total = total + lax.dot_general(
                    held[h, qq].reshape(rows, half),
                    wd[cols, h * half : (h + 1) * half],
                    (((1,), (1,)), ((), ())),
                    preferred_element_type=jnp.float32,
                )
            own_sum[g % 2, :, cols] = total
            half_out[g, :, cols] = total.astype(jnp.bfloat16)

        hc.append(go(remote(half_out.at[g], half_in.at[g], hs.at[g], hr.at[g], other)))

    def finish(g, qq):
        hc[g].wait_recv()

        @pl.loop(0, zl)
        def _(zi):
            part = pl.ds(pl.multiple_of(zi * tok, tok), tok)
            summed = own_sum[g % 2, part, :] + half_in[g, part, :].astype(jnp.float32)
            summed = summed * info[zi * 4 + qq, :, 0:1]
            gate = gate_tok[qq, zi].astype(jnp.float32)
            up = up_tok[qq, zi].astype(jnp.float32)
            sig = jax.nn.sigmoid(gate)
            grad_g[part, :] = (summed * up * (sig * (1.0 + gate * (1.0 - sig)))).astype(jnp.bfloat16)
            grad_u[part, :] = (summed * gate * sig).astype(jnp.bfloat16)

        for h in range(2):

            @pl.loop(0, half // 256)
            def _(n):
                wrows = pl.ds(pl.multiple_of(h * half + n * 256, 256), 256)
                cols = pl.ds(pl.multiple_of(n * 256, 256), 256)
                total = jnp.zeros((rows, 256), jnp.float32)
                for grad, weight in ((grad_g, wg), (grad_u, wu)):
                    total = total + lax.dot_general(
                        grad[...], weight[wrows, :],
                        (((1,), (1,)), ((), ())),
                        preferred_element_type=jnp.float32,
                    )
                contrib[h, qq, :, :, cols] = total.reshape(zl, tok, 256).astype(jnp.bfloat16)

    order = (2, 1, 3, 0)
    c1, c2, c3 = {}, {}, {}

    def first(h, g, qq, device):
        for k in order:
            c1[h, g, k] = go(
                remote(
                    contrib.at[h, qq, zto[k]], l1.at[h, g, k],
                    s1.at[h * 2 + g, k], r1.at[h * 2 + g, k], device,
                )
            )

    hidden(0, q)
    forward(2)
    for k in range(4):
        xc[k, 1].wait_recv()
    hidden(1, qx)
    finish(0, q)
    for k in range(4):
        yc[k, 0].wait_recv()
    hidden(2, qy)
    finish(1, qx)
    first(1, 0, qx, xn)
    for k in range(4):
        fc[k, 0].wait_recv()
        fc[k, 1].wait_recv()
    hidden(3, qd)
    finish(2, qy)
    first(0, 0, qy, yn)
    finish(3, qd)
    first(0, 1, qd, yn)
    first(1, 1, qd, xn)

    step = 32

    def add(dest, parts):
        @pl.loop(0, tok // step)
        def _(i):
            part = pl.ds(pl.multiple_of(i * step, step), step)
            dest(part, sum(p(part).astype(jnp.float32) for p in parts))

    def combine(h, qq, zi, parts):
        def store(part, value):
            contrib[h, qq, zi, part, :] = value.astype(jnp.bfloat16)

        add(store, [lambda part: contrib[h, qq, zi, part, :]] + parts)

    def second(k):
        for h, qq, device in ((0, qx, xn), (1, qy, yn)):
            c1[h, 1, k].wait_recv()
            combine(h, qq, zto[k], [lambda part: l1[h, 1, k, part, :]])
            c2[h, k] = go(
                remote(contrib.at[h, qq, zto[k]], l2.at[h, k], s2.at[h, k], r2.at[h, k], device)
            )

    def third(k):
        for h in range(2):
            c1[h, 0, k].wait_recv()
            c2[h, k].wait_recv()
            if k:
                combine(
                    h, q, zto[k],
                    [lambda part: l1[h, 0, k, part, :], lambda part: l2[h, k, part, :]],
                )
                c3[h, k] = go(
                    remote(contrib.at[h, q, zto[k]], l3.at[h, k], s3.at[h, k], r3.at[h, k], zdev[k])
                )

    second(order[0])
    second(order[1])
    third(order[0])
    second(order[2])
    third(order[1])
    second(order[3])
    third(order[2])
    third(order[3])
    for h in range(2):
        for k in (1, 2, 3):
            c3[h, k].wait_recv()

        def store(part, value):
            out[part, h * half : (h + 1) * half] = value.astype(jnp.bfloat16)

        add(
            store,
            [
                lambda part: contrib[h, q, z, part, :],
                lambda part: l1[h, 0, 0, part, :],
                lambda part: l2[h, 0, part, :],
                lambda part: l3[h, 1, part, :],
                lambda part: l3[h, 2, part, :],
                lambda part: l3[h, 3, part, :],
                lambda part: og[part, h * half : (h + 1) * half],
            ],
        )
    for copy in started:
        copy.wait_send()


def per_device_tokens(
    output_grad,
    gate_values,
    expert_ids,
    pre_gate,
    pre_up,
    w_gate,
    w_up,
    w_down,
    visual,
    visual_rows,
):
    tok, width = output_grad.shape
    half = width // 2
    experts = lax.axis_size("expert")
    capacity, hid = pre_gate.shape[2:]
    named = expert_ids[:, :, None] == jnp.arange(experts, dtype=jnp.int32)
    weight = jnp.sum(jnp.where(named, gate_values[:, :, None], 0.0), axis=1)
    here = jnp.any(named, axis=1)
    count = here.astype(jnp.int32)
    position = jnp.where(here, jnp.cumsum(count, axis=0) - count, -1).astype(jnp.float32)
    info = jnp.stack([weight.T, position.T], axis=1)
    info = lax.all_to_all(info, "expert", split_axis=0, concat_axis=0, tiled=True)
    info = jnp.transpose(info, (0, 2, 1))
    bf, dma = jnp.bfloat16, pltpu.SemaphoreType.DMA
    rows = 4 * tok
    input_grad = pl.pallas_call(
        expert_kernel,
        out_shape=jax.ShapeDtypeStruct((tok, width), bf),
        in_specs=[pl.BlockSpec(memory_space=pltpu.VMEM)] * 7,
        out_specs=pl.BlockSpec(memory_space=pltpu.VMEM),
        scratch_shapes=[
            pltpu.VMEM((2, 4, 4, tok, half), bf),
            pltpu.VMEM((2, 4, 4, tok, half), bf),
            pltpu.VMEM((4, 4, tok, hid), bf),
            pltpu.VMEM((4, 4, tok, hid), bf),
            pltpu.VMEM((2, rows, hid), jnp.float32),
            pltpu.VMEM((4, rows, hid), bf),
            pltpu.VMEM((4, rows, hid), bf),
            pltpu.VMEM((rows, hid), bf),
            pltpu.VMEM((rows, hid), bf),
            pltpu.VMEM((2, 2, 4, tok, half), bf),
            pltpu.VMEM((2, 4, tok, half), bf),
            pltpu.VMEM((2, 4, tok, half), bf),
        ]
        + [dma((4, 2))] * 8
        + [dma((4,))] * 2
        + [dma((4, 4))] * 2
        + [dma((2, 4))] * 4,
        compiler_params=pltpu.CompilerParams(
            collective_id=0, has_side_effects=True, vmem_limit_bytes=63 * 1024 * 1024
        ),
        cost_estimate=pl.CostEstimate(
            flops=6 * 4 * rows * width * hid, bytes_accessed=20 * 1024 * 1024, transcendentals=0
        ),
    )(
        output_grad, info,
        pre_gate[0].reshape(4, 4, capacity, hid), pre_up[0].reshape(4, 4, capacity, hid),
        w_gate[0], w_up[0], w_down[0],
    )
    return (input_grad, projector(input_grad, visual, visual_rows))


def projector(input_grad, visual, visual_rows):
    visual_grad = input_grad[visual_rows]
    features = lax.all_to_all(visual, "expert", split_axis=1, concat_axis=0, tiled=True)
    return jnp.einsum(
        "rv,rd->vd",
        features,
        lax.all_gather(visual_grad, "expert", axis=0, tiled=True),
        preferred_element_type=jnp.float32,
    )


def solution(mesh):
    per_rank = per_device_tokens if mesh.shape["expert"] == 16 else per_device
    in_specs = (
        P(("groups", "expert"), "tower"),
        P(("groups", "expert"), None),
        P(("groups", "expert"), None),
        P(("groups", "expert"), None, None, None),
        P(("groups", "expert"), None, None, None),
        P("expert", "tower", None),
        P("expert", "tower", None),
        P("expert", None, "tower"),
        P(("groups", "expert"), None),
        P(("groups", "expert")),
    )
    out_specs = (P(("groups", "expert"), "tower"), P(("groups", "expert"), "tower"))
    return jax.shard_map(
        per_rank, mesh=mesh, in_specs=in_specs, out_specs=out_specs, check_vma=False
    )
```

```python
import jax
import jax.numpy as jnp
from jax import lax
from jax.experimental import pallas as pl
from jax.experimental.pallas import tpu as pltpu
from jax.sharding import PartitionSpec as P


def hidden_grads(summed, gate_pre, up_pre):
    gate_float = gate_pre.astype(jnp.float32)
    up_float = up_pre.astype(jnp.float32)
    sigmoid_gate = jax.nn.sigmoid(gate_float)
    slope = sigmoid_gate * (1.0 + gate_float * (1.0 - sigmoid_gate))
    grad_gate = (summed * up_float * slope).astype(jnp.bfloat16)
    grad_up = (summed * gate_float * sigmoid_gate).astype(jnp.bfloat16)
    return (grad_gate, grad_up)


def per_device(
    output_grad,
    gate_values,
    expert_ids,
    pre_gate,
    pre_up,
    w_gate,
    w_up,
    w_down,
    visual,
    visual_rows,
):
    tok_rows, half_width = output_grad.shape
    top_count = expert_ids.shape[1]
    expert_count = lax.axis_size("expert")
    capacity = pre_gate.shape[2]
    hidden_units = pre_gate.shape[3]
    flat_ids = expert_ids.reshape(-1)
    onehot = (flat_ids[:, None] == jnp.arange(expert_count, dtype=jnp.int32)[None, :]).astype(
        jnp.int32
    )
    earlier = jnp.cumsum(onehot, axis=0) - onehot
    position = jnp.sum(earlier * onehot, axis=1)
    slot_index = flat_ids * capacity + position
    token_index = jnp.repeat(jnp.arange(tok_rows, dtype=jnp.int32), top_count)
    outgoing = (
        jnp.zeros((expert_count * capacity, half_width), jnp.bfloat16)
        .at[slot_index]
        .set(output_grad[token_index])
    )
    outgoing = outgoing.reshape(expert_count, capacity, half_width)
    incoming = lax.all_to_all(outgoing, "expert", split_axis=0, concat_axis=0, tiled=True)
    routed = incoming.reshape(-1, half_width)
    partial_value = jnp.einsum("rd,fd->rf", routed, w_down[0], preferred_element_type=jnp.float32)
    gate_pre = pre_gate[0].reshape(-1, hidden_units)
    up_pre = pre_up[0].reshape(-1, hidden_units)
    summed = lax.psum(partial_value, "tower")
    grad_gate, grad_up = hidden_grads(summed, gate_pre, up_pre)
    returning = jnp.einsum("rf,df->rd", grad_gate, w_gate[0], preferred_element_type=jnp.float32)
    returning = returning + jnp.einsum(
        "rf,df->rd", grad_up, w_up[0], preferred_element_type=jnp.float32
    )
    returning = returning.astype(jnp.bfloat16).reshape(expert_count, capacity, half_width)
    returned = lax.all_to_all(returning, "expert", split_axis=0, concat_axis=0, tiled=True)
    picked = returned.reshape(-1, half_width)[slot_index].reshape(tok_rows, top_count, half_width)
    combined = output_grad.astype(jnp.float32) + jnp.sum(
        gate_values[:, :, None] * picked.astype(jnp.float32), axis=1
    )
    input_grad = combined.astype(jnp.bfloat16)
    visual_grad = input_grad[visual_rows]
    features = lax.all_to_all(visual, "expert", split_axis=1, concat_axis=0, tiled=True)
    projector_grad = jnp.einsum(
        "rv,rd->vd",
        features,
        lax.all_gather(visual_grad, "expert", axis=0, tiled=True),
        preferred_element_type=jnp.float32,
    )
    return (input_grad, projector_grad)


def expert_kernel(
    og, info, pg, pu, wg, wu, wd, visual, vrows, out, vgrad_out, vis_out,
    held, contrib, gate_tok, up_tok, own_sum, half_out, half_in, grad_g, grad_u, l1, l2, l3,
    zs, zr, xs, xr, ys, yr, fs, fr, hs, hr, s1, r1, s2, r2, s3, r3,
    vis, vgrad, vs, vr, gs, gr,
):
    zl, tok, half = held.shape[2:]
    hid = wd.shape[0]
    cap = pg.shape[2]
    rows = zl * tok
    group, me, core = lax.axis_index("groups"), lax.axis_index("expert"), lax.axis_index("tower")
    z, y, x = lax.div(me, 4), lax.rem(lax.div(me, 2), 2), lax.rem(me, 2)
    q, qx = y * 2 + x, y * 2 + 1 - x
    qy, qd = (1 - y) * 2 + x, (1 - y) * 2 + 1 - x

    def dev(e):
        return (group, e, core)

    xn, yn = dev(z * 4 + qx), dev(z * 4 + qy)
    other = (group, me, 1 - core)
    zto = [lax.rem(z + k, 4) for k in range(4)]
    zfrom = [lax.rem(z + 4 - k, 4) for k in range(4)]
    zdev = [dev(zto[k] * 4 + q) for k in range(4)]

    def remote(src, dst, ss, rs, device):
        return pltpu.make_async_remote_copy(
            src_ref=src, dst_ref=dst, send_sem=ss, recv_sem=rs,
            device_id=device, device_id_type=pl.DeviceIdType.MESH,
        )

    barrier = pltpu.get_barrier_semaphore()
    for device in (xn, yn, other, zdev[1], zdev[2], zdev[3]):
        pl.semaphore_signal(barrier, inc=1, device_id=device, device_id_type=pl.DeviceIdType.MESH)
    for h in range(2):
        held[h, q, z] = og[:, h * half : (h + 1) * half]
    vis[q, z] = visual[...]
    pl.semaphore_wait(barrier, 6)

    started = []

    def go(copy):
        copy.start()
        started.append(copy)
        return copy

    def to_x(k, h):
        block = held.at[h, q, zfrom[k]]
        return go(remote(block, block, xs.at[k, h], xr.at[k, h], xn))

    def to_y(k, h):
        block = held.at[h, q, zfrom[k]]
        return go(remote(block, block, ys.at[k, h], yr.at[k, h], yn))

    def along_z(buf, ss, rs):
        block = buf.at[q, z]
        return [go(remote(block, block, ss.at[k - 1], rs.at[k - 1], zdev[k])) for k in (1, 2, 3)]

    def across(buf, ss, rs, copies):
        for copy in copies:
            copy.wait_recv()
        line = buf.at[q]
        return [
            go(remote(line, line, ss.at[3], rs.at[3], xn)),
            go(remote(line, line, ss.at[4], rs.at[4], yn)),
        ]

    def diagonal(buf, ss, rs, copies):
        for copy in copies:
            copy.wait_recv()
        low, high = buf.at[qx, pl.ds(0, 2)], buf.at[qy, pl.ds(2, 2)]
        return [
            go(remote(low, low, ss.at[5], rs.at[5], yn)),
            go(remote(high, high, ss.at[6], rs.at[6], xn)),
        ]

    zc, xc, yc, fc = {}, {}, {}, {}

    def forward(k):
        xc[k, 0].wait_recv()
        block = held.at[0, qx, zfrom[k]]
        fc[k, 0] = go(remote(block, block, fs.at[k, 0], fr.at[k, 0], yn))
        yc[k, 1].wait_recv()
        block = held.at[1, qy, zfrom[k]]
        fc[k, 1] = go(remote(block, block, fs.at[k, 1], fr.at[k, 1], xn))

    for k in (1, 3, 2):
        for h in range(2):
            block = held.at[h, q, z]
            zc[k, h] = remote(block, block, zs.at[k, h], zr.at[k, h], zdev[k])
    xc[0, 0], yc[0, 1] = to_x(0, 0), to_y(0, 1)
    for k in (1, 3, 2):
        go(zc[k, 0])
        go(zc[k, 1])
    xc[0, 1], yc[0, 0] = to_x(0, 1), to_y(0, 0)
    vc = along_z(vis, vs, vr)

    @pl.loop(0, 4)
    def _(zi):
        @pl.loop(0, 4)
        def _(qi):
            place = info[zi * 4 + qi, :, 1:2]
            slot = lax.broadcasted_iota(jnp.int32, (tok, cap), 1).astype(jnp.float32)
            spread = jnp.where(place == slot, 1.0, 0.0).astype(jnp.bfloat16)
            for pre, dest in ((pg, gate_tok), (pu, up_tok)):
                dest[qi, zi] = jnp.dot(
                    spread, pre[zi, qi], preferred_element_type=jnp.float32
                ).astype(jnp.bfloat16)

    done = None
    for k in (1, 3, 2):
        zc[k, 0].wait_recv()
        xc[k, 0] = to_x(k, 0)
        zc[k, 1].wait_recv()
        yc[k, 1] = to_y(k, 1)
        xc[k, 1], yc[k, 0] = to_x(k, 1), to_y(k, 0)
        forward(0 if done is None else done)
        done = k

    hc = []

    def hidden(g, qq):
        @pl.loop(0, hid // 256)
        def _(n):
            cols = pl.ds(pl.multiple_of(n * 256, 256), 256)
            total = jnp.zeros((rows, 256), jnp.float32)
            for h in range(2):
                total = total + lax.dot_general(
                    held[h, qq].reshape(rows, half),
                    wd[cols, h * half : (h + 1) * half],
                    (((1,), (1,)), ((), ())),
                    preferred_element_type=jnp.float32,
                )
            own_sum[g % 2, :, cols] = total
            half_out[g, :, cols] = total.astype(jnp.bfloat16)

        hc.append(go(remote(half_out.at[g], half_in.at[g], hs.at[g], hr.at[g], other)))

    def finish(g, qq):
        hc[g].wait_recv()

        @pl.loop(0, zl)
        def _(zi):
            part = pl.ds(pl.multiple_of(zi * tok, tok), tok)
            summed = own_sum[g % 2, part, :] + half_in[g, part, :].astype(jnp.float32)
            summed = summed * info[zi * 4 + qq, :, 0:1]
            gate = gate_tok[qq, zi].astype(jnp.float32)
            up = up_tok[qq, zi].astype(jnp.float32)
            sig = jax.nn.sigmoid(gate)
            grad_g[part, :] = (summed * up * (sig * (1.0 + gate * (1.0 - sig)))).astype(jnp.bfloat16)
            grad_u[part, :] = (summed * gate * sig).astype(jnp.bfloat16)

        for h in range(2):

            @pl.loop(0, half // 256)
            def _(n):
                wrows = pl.ds(pl.multiple_of(h * half + n * 256, 256), 256)
                cols = pl.ds(pl.multiple_of(n * 256, 256), 256)
                total = jnp.zeros((rows, 256), jnp.float32)
                for grad, weight in ((grad_g, wg), (grad_u, wu)):
                    total = total + lax.dot_general(
                        grad[...], weight[wrows, :],
                        (((1,), (1,)), ((), ())),
                        preferred_element_type=jnp.float32,
                    )
                contrib[h, qq, :, :, cols] = total.reshape(zl, tok, 256).astype(jnp.bfloat16)

    order = (2, 1, 3, 0)
    c1, c2, c3 = {}, {}, {}

    def first(h, g, qq, device):
        for k in order:
            c1[h, g, k] = go(
                remote(
                    contrib.at[h, qq, zto[k]], l1.at[h, g, k],
                    s1.at[h * 2 + g, k], r1.at[h * 2 + g, k], device,
                )
            )

    vc = across(vis, vs, vr, vc)
    hidden(0, q)
    forward(2)
    for k in range(4):
        xc[k, 1].wait_recv()
    hidden(1, qx)
    finish(0, q)
    for k in range(4):
        yc[k, 0].wait_recv()
    hidden(2, qy)
    finish(1, qx)
    first(1, 0, qx, xn)
    for k in range(4):
        fc[k, 0].wait_recv()
        fc[k, 1].wait_recv()
    vc = diagonal(vis, vs, vr, vc)
    hidden(3, qd)
    finish(2, qy)
    first(0, 0, qy, yn)
    finish(3, qd)
    first(0, 1, qd, yn)
    first(1, 1, qd, xn)

    step = 32

    def add(dest, parts):
        @pl.loop(0, tok // step)
        def _(i):
            part = pl.ds(pl.multiple_of(i * step, step), step)
            dest(part, sum(p(part).astype(jnp.float32) for p in parts))

    def combine(h, qq, zi, parts):
        def store(part, value):
            contrib[h, qq, zi, part, :] = value.astype(jnp.bfloat16)

        add(store, [lambda part: contrib[h, qq, zi, part, :]] + parts)

    def second(k):
        for h, qq, device in ((0, qx, xn), (1, qy, yn)):
            c1[h, 1, k].wait_recv()
            combine(h, qq, zto[k], [lambda part: l1[h, 1, k, part, :]])
            c2[h, k] = go(
                remote(contrib.at[h, qq, zto[k]], l2.at[h, k], s2.at[h, k], r2.at[h, k], device)
            )

    def third(k):
        for h in range(2):
            c1[h, 0, k].wait_recv()
            c2[h, k].wait_recv()
            if k:
                combine(
                    h, q, zto[k],
                    [lambda part: l1[h, 0, k, part, :], lambda part: l2[h, k, part, :]],
                )
                c3[h, k] = go(
                    remote(contrib.at[h, q, zto[k]], l3.at[h, k], s3.at[h, k], r3.at[h, k], zdev[k])
                )

    second(order[0])
    second(order[1])
    third(order[0])
    second(order[2])
    third(order[1])
    second(order[3])
    third(order[2])
    third(order[3])
    for h in range(2):
        for k in (1, 2, 3):
            c3[h, k].wait_recv()

        def store(part, value):
            out[part, h * half : (h + 1) * half] = value.astype(jnp.bfloat16)

        add(
            store,
            [
                lambda part: contrib[h, q, z, part, :],
                lambda part: l1[h, 0, 0, part, :],
                lambda part: l2[h, 0, part, :],
                lambda part: l3[h, 1, part, :],
                lambda part: l3[h, 2, part, :],
                lambda part: l3[h, 3, part, :],
                lambda part: og[part, h * half : (h + 1) * half],
            ],
        )
    choice = vrows[...] == lax.broadcasted_iota(jnp.int32, (vrows.shape[0], tok), 1)
    choice = jnp.where(choice, 1.0, 0.0).astype(jnp.bfloat16)
    for c in range(0, 2 * half, 512):
        vgrad[q, z, :, c : c + 512] = jnp.dot(
            choice, out[:, c : c + 512], preferred_element_type=jnp.float32
        ).astype(jnp.bfloat16)
    gc = across(vgrad, gs, gr, along_z(vgrad, gs, gr))
    for copy in vc:
        copy.wait_recv()
    vis_out[...] = vis[...]
    for copy in diagonal(vgrad, gs, gr, gc):
        copy.wait_recv()
    vgrad_out[...] = vgrad[...]
    for copy in started:
        copy.wait_send()


def per_device_tokens(
    output_grad,
    gate_values,
    expert_ids,
    pre_gate,
    pre_up,
    w_gate,
    w_up,
    w_down,
    visual,
    visual_rows,
):
    tok, width = output_grad.shape
    half = width // 2
    experts = lax.axis_size("expert")
    capacity, hid = pre_gate.shape[2:]
    named = expert_ids[:, :, None] == jnp.arange(experts, dtype=jnp.int32)
    weight = jnp.sum(jnp.where(named, gate_values[:, :, None], 0.0), axis=1)
    here = jnp.any(named, axis=1)
    count = here.astype(jnp.int32)
    position = jnp.where(here, jnp.cumsum(count, axis=0) - count, -1).astype(jnp.float32)
    info = jnp.stack([weight.T, position.T], axis=1)
    info = lax.all_to_all(info, "expert", split_axis=0, concat_axis=0, tiled=True)
    info = jnp.transpose(info, (0, 2, 1))
    bf, dma = jnp.bfloat16, pltpu.SemaphoreType.DMA
    rows = 4 * tok
    vis_rows, vis_width = visual.shape
    input_grad, vgrad, vis = pl.pallas_call(
        expert_kernel,
        out_shape=(
            jax.ShapeDtypeStruct((tok, width), bf),
            jax.ShapeDtypeStruct((4, 4, vis_rows, width), bf),
            jax.ShapeDtypeStruct((4, 4, vis_rows, vis_width), bf),
        ),
        in_specs=[pl.BlockSpec(memory_space=pltpu.VMEM)] * 9,
        out_specs=(pl.BlockSpec(memory_space=pltpu.VMEM),) * 3,
        scratch_shapes=[
            pltpu.VMEM((2, 4, 4, tok, half), bf),
            pltpu.VMEM((2, 4, 4, tok, half), bf),
            pltpu.VMEM((4, 4, tok, hid), bf),
            pltpu.VMEM((4, 4, tok, hid), bf),
            pltpu.VMEM((2, rows, hid), jnp.float32),
            pltpu.VMEM((4, rows, hid), bf),
            pltpu.VMEM((4, rows, hid), bf),
            pltpu.VMEM((rows, hid), bf),
            pltpu.VMEM((rows, hid), bf),
            pltpu.VMEM((2, 2, 4, tok, half), bf),
            pltpu.VMEM((2, 4, tok, half), bf),
            pltpu.VMEM((2, 4, tok, half), bf),
        ]
        + [dma((4, 2))] * 8
        + [dma((4,))] * 2
        + [dma((4, 4))] * 2
        + [dma((2, 4))] * 4
        + [
            pltpu.VMEM((4, 4, vis_rows, vis_width), bf),
            pltpu.VMEM((4, 4, vis_rows, width), bf),
        ]
        + [dma((7,))] * 4,
        compiler_params=pltpu.CompilerParams(
            collective_id=0, has_side_effects=True, vmem_limit_bytes=63 * 1024 * 1024
        ),
        cost_estimate=pl.CostEstimate(
            flops=6 * 4 * rows * width * hid, bytes_accessed=20 * 1024 * 1024, transcendentals=0
        ),
    )(
        output_grad, info,
        pre_gate[0].reshape(4, 4, capacity, hid), pre_up[0].reshape(4, 4, capacity, hid),
        w_gate[0], w_up[0], w_down[0], visual, visual_rows[:, None],
    )
    share = vis_width // experts
    features = lax.dynamic_slice_in_dim(
        vis.reshape(-1, vis_width), lax.axis_index("expert") * share, share, axis=1
    )
    projector_grad = jnp.einsum(
        "rv,rd->vd", features, vgrad.reshape(-1, width), preferred_element_type=jnp.float32
    )
    return (input_grad, projector_grad)


def solution(mesh):
    per_rank = per_device_tokens if mesh.shape["expert"] == 16 else per_device
    in_specs = (
        P(("groups", "expert"), "tower"),
        P(("groups", "expert"), None),
        P(("groups", "expert"), None),
        P(("groups", "expert"), None, None, None),
        P(("groups", "expert"), None, None, None),
        P("expert", "tower", None),
        P("expert", "tower", None),
        P("expert", None, "tower"),
        P(("groups", "expert"), None),
        P(("groups", "expert")),
    )
    out_specs = (P(("groups", "expert"), "tower"), P(("groups", "expert"), "tower"))
    return jax.shard_map(
        per_rank, mesh=mesh, in_specs=in_specs, out_specs=out_specs, check_vma=False
    )
```

```python
import jax
import jax.numpy as jnp
from jax import lax
from jax.experimental import pallas as pl
from jax.experimental.pallas import tpu as pltpu
from jax.sharding import PartitionSpec as P


def hidden_grads(summed, gate_pre, up_pre):
    gate_float = gate_pre.astype(jnp.float32)
    up_float = up_pre.astype(jnp.float32)
    sigmoid_gate = jax.nn.sigmoid(gate_float)
    slope = sigmoid_gate * (1.0 + gate_float * (1.0 - sigmoid_gate))
    grad_gate = (summed * up_float * slope).astype(jnp.bfloat16)
    grad_up = (summed * gate_float * sigmoid_gate).astype(jnp.bfloat16)
    return (grad_gate, grad_up)


def per_device(
    output_grad,
    gate_values,
    expert_ids,
    pre_gate,
    pre_up,
    w_gate,
    w_up,
    w_down,
    visual,
    visual_rows,
):
    tok_rows, half_width = output_grad.shape
    top_count = expert_ids.shape[1]
    expert_count = lax.axis_size("expert")
    capacity = pre_gate.shape[2]
    hidden_units = pre_gate.shape[3]
    flat_ids = expert_ids.reshape(-1)
    onehot = (flat_ids[:, None] == jnp.arange(expert_count, dtype=jnp.int32)[None, :]).astype(
        jnp.int32
    )
    earlier = jnp.cumsum(onehot, axis=0) - onehot
    position = jnp.sum(earlier * onehot, axis=1)
    slot_index = flat_ids * capacity + position
    token_index = jnp.repeat(jnp.arange(tok_rows, dtype=jnp.int32), top_count)
    outgoing = (
        jnp.zeros((expert_count * capacity, half_width), jnp.bfloat16)
        .at[slot_index]
        .set(output_grad[token_index])
    )
    outgoing = outgoing.reshape(expert_count, capacity, half_width)
    incoming = lax.all_to_all(outgoing, "expert", split_axis=0, concat_axis=0, tiled=True)
    routed = incoming.reshape(-1, half_width)
    partial_value = jnp.einsum("rd,fd->rf", routed, w_down[0], preferred_element_type=jnp.float32)
    gate_pre = pre_gate[0].reshape(-1, hidden_units)
    up_pre = pre_up[0].reshape(-1, hidden_units)
    summed = lax.psum(partial_value, "tower")
    grad_gate, grad_up = hidden_grads(summed, gate_pre, up_pre)
    returning = jnp.einsum("rf,df->rd", grad_gate, w_gate[0], preferred_element_type=jnp.float32)
    returning = returning + jnp.einsum(
        "rf,df->rd", grad_up, w_up[0], preferred_element_type=jnp.float32
    )
    returning = returning.astype(jnp.bfloat16).reshape(expert_count, capacity, half_width)
    returned = lax.all_to_all(returning, "expert", split_axis=0, concat_axis=0, tiled=True)
    picked = returned.reshape(-1, half_width)[slot_index].reshape(tok_rows, top_count, half_width)
    combined = output_grad.astype(jnp.float32) + jnp.sum(
        gate_values[:, :, None] * picked.astype(jnp.float32), axis=1
    )
    input_grad = combined.astype(jnp.bfloat16)
    visual_grad = input_grad[visual_rows]
    features = lax.all_to_all(visual, "expert", split_axis=1, concat_axis=0, tiled=True)
    projector_grad = jnp.einsum(
        "rv,rd->vd",
        features,
        lax.all_gather(visual_grad, "expert", axis=0, tiled=True),
        preferred_element_type=jnp.float32,
    )
    return (input_grad, projector_grad)


def expert_kernel(
    og, info_own, pg, pu, wg, wu, wd, visual, vrows, out, vgrad_out, vis_out,
    held, contrib, gate_tok, up_tok, own_sum, half_out, half_in, grad_g, grad_u, l1, l2, l3,
    zs, zr, xs, xr, ys, yr, fs, fr, hs, hr, s1, r1, s2, r2, s3, r3,
    vis, vgrad, vs, vr, gs, gr, info, ns, nr,
):
    zl, tok, half = held.shape[2:]
    hid = wd.shape[0]
    cap = pg.shape[2]
    rows = zl * tok
    group, me, core = lax.axis_index("groups"), lax.axis_index("expert"), lax.axis_index("tower")
    z, y, x = lax.div(me, 4), lax.rem(lax.div(me, 2), 2), lax.rem(me, 2)
    q, qx = y * 2 + x, y * 2 + 1 - x
    qy, qd = (1 - y) * 2 + x, (1 - y) * 2 + 1 - x

    def dev(e):
        return (group, e, core)

    xn, yn = dev(z * 4 + qx), dev(z * 4 + qy)
    other = (group, me, 1 - core)
    zto = [lax.rem(z + k, 4) for k in range(4)]
    zfrom = [lax.rem(z + 4 - k, 4) for k in range(4)]
    zdev = [dev(zto[k] * 4 + q) for k in range(4)]

    def remote(src, dst, ss, rs, device):
        return pltpu.make_async_remote_copy(
            src_ref=src, dst_ref=dst, send_sem=ss, recv_sem=rs,
            device_id=device, device_id_type=pl.DeviceIdType.MESH,
        )

    barrier = pltpu.get_barrier_semaphore()
    for device in (xn, yn, other, zdev[1], zdev[2], zdev[3]):
        pl.semaphore_signal(barrier, inc=1, device_id=device, device_id_type=pl.DeviceIdType.MESH)
    for h in range(2):
        held[h, q, z] = og[:, h * half : (h + 1) * half]
    vis[q, z] = visual[...]
    info[q, z] = info_own[...]
    pl.semaphore_wait(barrier, 6)

    started = []

    def go(copy):
        copy.start()
        started.append(copy)
        return copy

    def to_x(k, h):
        block = held.at[h, q, zfrom[k]]
        return go(remote(block, block, xs.at[k, h], xr.at[k, h], xn))

    def to_y(k, h):
        block = held.at[h, q, zfrom[k]]
        return go(remote(block, block, ys.at[k, h], yr.at[k, h], yn))

    def along_z(buf, ss, rs):
        block = buf.at[q, z]
        return [go(remote(block, block, ss.at[k - 1], rs.at[k - 1], zdev[k])) for k in (1, 2, 3)]

    def across(buf, ss, rs, copies):
        for copy in copies:
            copy.wait_recv()
        line = buf.at[q]
        return [
            go(remote(line, line, ss.at[3], rs.at[3], xn)),
            go(remote(line, line, ss.at[4], rs.at[4], yn)),
        ]

    def diagonal(buf, ss, rs, copies):
        for copy in copies:
            copy.wait_recv()
        low, high = buf.at[qx, pl.ds(0, 2)], buf.at[qy, pl.ds(2, 2)]
        return [
            go(remote(low, low, ss.at[5], rs.at[5], yn)),
            go(remote(high, high, ss.at[6], rs.at[6], xn)),
        ]

    zc, xc, yc, fc = {}, {}, {}, {}

    def forward(k):
        xc[k, 0].wait_recv()
        block = held.at[0, qx, zfrom[k]]
        fc[k, 0] = go(remote(block, block, fs.at[k, 0], fr.at[k, 0], yn))
        yc[k, 1].wait_recv()
        block = held.at[1, qy, zfrom[k]]
        fc[k, 1] = go(remote(block, block, fs.at[k, 1], fr.at[k, 1], xn))

    for k in (1, 3, 2):
        for h in range(2):
            block = held.at[h, q, z]
            zc[k, h] = remote(block, block, zs.at[k, h], zr.at[k, h], zdev[k])
    nc = along_z(info, ns, nr)
    xc[0, 0], yc[0, 1] = to_x(0, 0), to_y(0, 1)
    for k in (1, 3, 2):
        go(zc[k, 0])
        go(zc[k, 1])
    xc[0, 1], yc[0, 0] = to_x(0, 1), to_y(0, 0)
    vc = along_z(vis, vs, vr)
    nc = across(info, ns, nr, nc)

    def pick(block, lane):
        lanes = lax.broadcasted_iota(jnp.int32, block.shape, 1)
        return jnp.sum(jnp.where(lanes == lane, block, 0.0), axis=1, keepdims=True)

    done = None
    for k in (1, 3, 2):
        zc[k, 0].wait_recv()
        xc[k, 0] = to_x(k, 0)
        zc[k, 1].wait_recv()
        yc[k, 1] = to_y(k, 1)
        xc[k, 1], yc[k, 0] = to_x(k, 1), to_y(k, 0)
        forward(0 if done is None else done)
        if done is None:
            nc = diagonal(info, ns, nr, nc)
        done = k

    hc = []

    def hidden(g, qq):
        @pl.loop(0, hid // 256)
        def _(n):
            cols = pl.ds(pl.multiple_of(n * 256, 256), 256)
            total = jnp.zeros((rows, 256), jnp.float32)
            for h in range(2):
                total = total + lax.dot_general(
                    held[h, qq].reshape(rows, half),
                    wd[cols, h * half : (h + 1) * half],
                    (((1,), (1,)), ((), ())),
                    preferred_element_type=jnp.float32,
                )
            own_sum[g % 2, :, cols] = total
            half_out[g, :, cols] = total.astype(jnp.bfloat16)

        hc.append(go(remote(half_out.at[g], half_in.at[g], hs.at[g], hr.at[g], other)))

    def finish(g, qq):
        hc[g].wait_recv()

        @pl.loop(0, zl)
        def _(zi):
            part = pl.ds(pl.multiple_of(zi * tok, tok), tok)
            summed = own_sum[g % 2, part, :] + half_in[g, part, :].astype(jnp.float32)
            summed = summed * pick(info[qq, zi], me)
            gate = gate_tok[qq, zi].astype(jnp.float32)
            up = up_tok[qq, zi].astype(jnp.float32)
            sig = jax.nn.sigmoid(gate)
            grad_g[part, :] = (summed * up * (sig * (1.0 + gate * (1.0 - sig)))).astype(jnp.bfloat16)
            grad_u[part, :] = (summed * gate * sig).astype(jnp.bfloat16)

        for h in range(2):

            @pl.loop(0, half // 256)
            def _(n):
                wrows = pl.ds(pl.multiple_of(h * half + n * 256, 256), 256)
                cols = pl.ds(pl.multiple_of(n * 256, 256), 256)
                total = jnp.zeros((rows, 256), jnp.float32)
                for grad, weight in ((grad_g, wg), (grad_u, wu)):
                    total = total + lax.dot_general(
                        grad[...], weight[wrows, :],
                        (((1,), (1,)), ((), ())),
                        preferred_element_type=jnp.float32,
                    )
                contrib[h, qq, :, :, cols] = total.reshape(zl, tok, 256).astype(jnp.bfloat16)

    order = (2, 1, 3, 0)
    c1, c2, c3 = {}, {}, {}

    def first(h, g, qq, device):
        for k in order:
            c1[h, g, k] = go(
                remote(
                    contrib.at[h, qq, zto[k]], l1.at[h, g, k],
                    s1.at[h * 2 + g, k], r1.at[h * 2 + g, k], device,
                )
            )

    vc = across(vis, vs, vr, vc)
    for copy in nc:
        copy.wait_recv()

    @pl.loop(0, 4)
    def _(zi):
        @pl.loop(0, 4)
        def _(qi):
            place = pick(info[qi, zi], 16 + me)
            slot = lax.broadcasted_iota(jnp.int32, (tok, cap), 1).astype(jnp.float32)
            spread = jnp.where(place == slot, 1.0, 0.0).astype(jnp.bfloat16)
            for pre, dest in ((pg, gate_tok), (pu, up_tok)):
                dest[qi, zi] = jnp.dot(
                    spread, pre[zi, qi], preferred_element_type=jnp.float32
                ).astype(jnp.bfloat16)

    hidden(0, q)
    forward(2)
    for k in range(4):
        xc[k, 1].wait_recv()
    hidden(1, qx)
    finish(0, q)
    for k in range(4):
        yc[k, 0].wait_recv()
    hidden(2, qy)
    finish(1, qx)
    first(1, 0, qx, xn)
    for k in range(4):
        fc[k, 0].wait_recv()
        fc[k, 1].wait_recv()
    vc = diagonal(vis, vs, vr, vc)
    hidden(3, qd)
    finish(2, qy)
    first(0, 0, qy, yn)
    finish(3, qd)
    first(0, 1, qd, yn)
    first(1, 1, qd, xn)

    step = 32

    def add(dest, parts):
        @pl.loop(0, tok // step)
        def _(i):
            part = pl.ds(pl.multiple_of(i * step, step), step)
            dest(part, sum(p(part).astype(jnp.float32) for p in parts))

    def combine(h, qq, zi, parts):
        def store(part, value):
            contrib[h, qq, zi, part, :] = value.astype(jnp.bfloat16)

        add(store, [lambda part: contrib[h, qq, zi, part, :]] + parts)

    def second(k):
        for h, qq, device in ((0, qx, xn), (1, qy, yn)):
            c1[h, 1, k].wait_recv()
            combine(h, qq, zto[k], [lambda part: l1[h, 1, k, part, :]])
            c2[h, k] = go(
                remote(contrib.at[h, qq, zto[k]], l2.at[h, k], s2.at[h, k], r2.at[h, k], device)
            )

    def third(k):
        for h in range(2):
            c1[h, 0, k].wait_recv()
            c2[h, k].wait_recv()
            if k:
                combine(
                    h, q, zto[k],
                    [lambda part: l1[h, 0, k, part, :], lambda part: l2[h, k, part, :]],
                )
                c3[h, k] = go(
                    remote(contrib.at[h, q, zto[k]], l3.at[h, k], s3.at[h, k], r3.at[h, k], zdev[k])
                )

    second(order[0])
    second(order[1])
    third(order[0])
    second(order[2])
    third(order[1])
    second(order[3])
    third(order[2])
    third(order[3])
    for h in range(2):
        for k in (1, 2, 3):
            c3[h, k].wait_recv()

        def store(part, value):
            out[part, h * half : (h + 1) * half] = value.astype(jnp.bfloat16)

        add(
            store,
            [
                lambda part: contrib[h, q, z, part, :],
                lambda part: l1[h, 0, 0, part, :],
                lambda part: l2[h, 0, part, :],
                lambda part: l3[h, 1, part, :],
                lambda part: l3[h, 2, part, :],
                lambda part: l3[h, 3, part, :],
                lambda part: og[part, h * half : (h + 1) * half],
            ],
        )
    choice = vrows[...] == lax.broadcasted_iota(jnp.int32, (vrows.shape[0], tok), 1)
    choice = jnp.where(choice, 1.0, 0.0).astype(jnp.bfloat16)
    for c in range(0, 2 * half, 512):
        vgrad[q, z, :, c : c + 512] = jnp.dot(
            choice, out[:, c : c + 512], preferred_element_type=jnp.float32
        ).astype(jnp.bfloat16)
    gc = across(vgrad, gs, gr, along_z(vgrad, gs, gr))
    for copy in vc:
        copy.wait_recv()
    vis_out[...] = vis[...]
    for copy in diagonal(vgrad, gs, gr, gc):
        copy.wait_recv()
    vgrad_out[...] = vgrad[...]
    for copy in started:
        copy.wait_send()


def per_device_tokens(
    output_grad,
    gate_values,
    expert_ids,
    pre_gate,
    pre_up,
    w_gate,
    w_up,
    w_down,
    visual,
    visual_rows,
):
    tok, width = output_grad.shape
    half = width // 2
    experts = lax.axis_size("expert")
    capacity, hid = pre_gate.shape[2:]
    named = expert_ids[:, :, None] == jnp.arange(experts, dtype=jnp.int32)
    weight = jnp.sum(jnp.where(named, gate_values[:, :, None], 0.0), axis=1)
    here = jnp.any(named, axis=1)
    count = here.astype(jnp.int32)
    position = jnp.where(here, jnp.cumsum(count, axis=0) - count, -1).astype(jnp.float32)
    info = jnp.concatenate([weight, position], axis=1)
    info = jnp.pad(info, ((0, 0), (0, 128 - 2 * experts)))
    bf, dma = jnp.bfloat16, pltpu.SemaphoreType.DMA
    rows = 4 * tok
    vis_rows, vis_width = visual.shape
    input_grad, vgrad, vis = pl.pallas_call(
        expert_kernel,
        out_shape=(
            jax.ShapeDtypeStruct((tok, width), bf),
            jax.ShapeDtypeStruct((4, 4, vis_rows, width), bf),
            jax.ShapeDtypeStruct((4, 4, vis_rows, vis_width), bf),
        ),
        in_specs=[pl.BlockSpec(memory_space=pltpu.VMEM)] * 9,
        out_specs=(pl.BlockSpec(memory_space=pltpu.VMEM),) * 3,
        scratch_shapes=[
            pltpu.VMEM((2, 4, 4, tok, half), bf),
            pltpu.VMEM((2, 4, 4, tok, half), bf),
            pltpu.VMEM((4, 4, tok, hid), bf),
            pltpu.VMEM((4, 4, tok, hid), bf),
            pltpu.VMEM((2, rows, hid), jnp.float32),
            pltpu.VMEM((4, rows, hid), bf),
            pltpu.VMEM((4, rows, hid), bf),
            pltpu.VMEM((rows, hid), bf),
            pltpu.VMEM((rows, hid), bf),
            pltpu.VMEM((2, 2, 4, tok, half), bf),
            pltpu.VMEM((2, 4, tok, half), bf),
            pltpu.VMEM((2, 4, tok, half), bf),
        ]
        + [dma((4, 2))] * 8
        + [dma((4,))] * 2
        + [dma((4, 4))] * 2
        + [dma((2, 4))] * 4
        + [
            pltpu.VMEM((4, 4, vis_rows, vis_width), bf),
            pltpu.VMEM((4, 4, vis_rows, width), bf),
        ]
        + [dma((7,))] * 4
        + [pltpu.VMEM((4, 4, tok, 128), jnp.float32)]
        + [dma((7,))] * 2,
        compiler_params=pltpu.CompilerParams(
            collective_id=0, has_side_effects=True, vmem_limit_bytes=63 * 1024 * 1024
        ),
        cost_estimate=pl.CostEstimate(
            flops=6 * 4 * rows * width * hid, bytes_accessed=20 * 1024 * 1024, transcendentals=0
        ),
    )(
        output_grad, info,
        pre_gate[0].reshape(4, 4, capacity, hid), pre_up[0].reshape(4, 4, capacity, hid),
        w_gate[0], w_up[0], w_down[0], visual, visual_rows[:, None],
    )
    share = vis_width // experts
    features = lax.dynamic_slice_in_dim(
        vis.reshape(-1, vis_width), lax.axis_index("expert") * share, share, axis=1
    )
    projector_grad = jnp.einsum(
        "rv,rd->vd", features, vgrad.reshape(-1, width), preferred_element_type=jnp.float32
    )
    return (input_grad, projector_grad)


def solution(mesh):
    per_rank = per_device_tokens if mesh.shape["expert"] == 16 else per_device
    in_specs = (
        P(("groups", "expert"), "tower"),
        P(("groups", "expert"), None),
        P(("groups", "expert"), None),
        P(("groups", "expert"), None, None, None),
        P(("groups", "expert"), None, None, None),
        P("expert", "tower", None),
        P("expert", "tower", None),
        P("expert", None, "tower"),
        P(("groups", "expert"), None),
        P(("groups", "expert")),
    )
    out_specs = (P(("groups", "expert"), "tower"), P(("groups", "expert"), "tower"))
    return jax.shard_map(
        per_rank, mesh=mesh, in_specs=in_specs, out_specs=out_specs, check_vma=False
    )
```
